128 devices in a mesh: node: 32 (over z, y, core), pb: 4 (over x).
Axes of the slice: x: 4, y: 4, z: 4, core: 2. Of those that a mesh axis runs over, the one named last changes fastest.
Arguments:
- node_scores: bfloat16 [262144, 512], P('node', 'pb'), may hold values from -8 to 8
- seeds: int32 [512], P('pb'), may hold values from 0 to 262143
- node_lists: int32 [2048, 8], P('node'), may hold values from 0 to 127
- node_tiles: bfloat16 [2048, 8, 128, 128], P('node'), as said below
- anchor_lists: int32 [128, 4], replicated, may hold values from 0 to 127
- anchor_tiles: bfloat16 [128, 4, 128, 128], P('node'), as said below
Outputs:
- ranking: bfloat16 [262144, 512], P('node', 'pb')
- anchor_scores: float32 [16384, 512], P('node', 'pb')
The draws below stay inside these ranges and needn't reach their ends.
Inputs may be any that keep to these rules, and one draw needn't show every extreme that they name: `node_tiles`: entries of order 1 / sqrt(16384). `anchor_tiles`: entries of order 0.5 / sqrt(512).
All inputs are finite; a program needn't handle non-finite values.
Results may differ from the reference program's by a relative error of at most 0.011.
Values may be sent and summed in bfloat16 or wider, within the bound.
A program may use at most 192 MiB of HBM per device.

```python
import math
import jax
import jax.numpy as jnp
import numpy as np
from jax import lax

BLK = 128
Q = 512
KN = 8
KA = 4
ITERS = 2
NB_DEV = 64
AB_DEV = 4
NBLOCKS = 2048
NODES = 262144
ABLOCKS = 128
ANCHORS = 16384


def draw_node_scores(key, part):
    key = jax.random.fold_in(key, 11)
    first, second = jax.random.split(key)
    ramp = jnp.exp(jnp.linspace(0.0, math.log(2.0), Q)).astype(jnp.float32)
    base = jax.random.normal(first, (NODES, Q), jnp.float32)
    rough = jnp.exp(jax.random.uniform(second, (1, Q), jnp.float32, -0.3, 0.3))
    return jnp.clip(base * ramp[None, :] * rough, -8.0, 8.0).astype(jnp.bfloat16)


def draw_node_tiles(key, part):
    key = jax.random.fold_in(key, 23)
    scale = math.sqrt(AB_DEV / (NB_DEV * KN * BLK))
    shape = (NBLOCKS, KN, BLK, BLK)
    base = jnp.clip(jax.random.normal(key, shape, jnp.float32), -5.0, 5.0)
    return (scale * base).astype(jnp.bfloat16)


def draw_anchor_tiles(key, part):
    key = jax.random.fold_in(key, 37)
    scale = 0.5 / math.sqrt(KA * BLK)
    shape = (ABLOCKS, KA, BLK, BLK)
    base = jnp.clip(jax.random.normal(key, shape, jnp.float32), -5.0, 5.0)
    return (scale * base).astype(jnp.bfloat16)


def with_ends(entries, own_key, low, high):
    index_at = [jax.random.randint(jax.random.fold_in(own_key, axis), (), 0, length) for axis, length in enumerate(entries.shape)]
    widest = entries.shape.index(max(entries.shape))
    neighbour = index_at[:widest] + [(index_at[widest] + 1) % entries.shape[widest]] + index_at[widest + 1:]
    return entries.at[tuple(index_at)].set(low).at[tuple(neighbour)].set(high)


def rank_table(amount, slope):
    weights = [(1 << 20) // math.isqrt(rank ** slope) + 1 for rank in range(1, amount + 1)]
    deviation = 1 + sum(weights) // (1 << 30)
    return np.cumsum(np.array([max(1, weight // deviation) for weight in weights]))


def ranked_ids(own_key, shape, amount, lean):
    table = rank_table(amount, lean)
    pick = jax.random.randint(jax.random.fold_in(own_key, 1), shape, 0, int(table[amount - 1]))
    rank = jnp.searchsorted(jnp.asarray(table, jnp.int32), pick, side="right")
    return jax.random.permutation(jax.random.fold_in(own_key, 2), amount)[rank].astype(jnp.int32)


def setup_inputs(seed: int = 0) -> dict:
    streams_of = jax.random.split(jax.random.key(seed), 7)
    return {
        "node_scores": draw_node_scores(jax.random.fold_in(streams_of[6], 71), 0),
        "seeds": with_ends(jax.random.randint(streams_of[1], (Q,), 0, NODES), jax.random.fold_in(streams_of[1], 1), 0, NODES - 1).astype(jnp.int32),
        "node_lists": with_ends(ranked_ids(streams_of[2], (NBLOCKS, KN), ABLOCKS, 1), jax.random.fold_in(streams_of[2], 3), 0, ABLOCKS - 1).astype(jnp.int32),
        "node_tiles": draw_node_tiles(jax.random.fold_in(streams_of[6], 71), 0),
        "anchor_lists": with_ends(jax.random.randint(streams_of[4], (ABLOCKS, KA), 0, ABLOCKS), jax.random.fold_in(streams_of[4], 1), 0, ABLOCKS - 1).astype(jnp.int32),
        "anchor_tiles": draw_anchor_tiles(jax.random.fold_in(streams_of[6], 71), 0),
    }


SEED_GAIN = 4.0
EPS = 1e-05

def reference(node_scores, seeds, node_lists, node_tiles, anchor_lists, anchor_tiles):
    rows = jnp.arange(NODES, dtype=jnp.int32)
    hit = (rows[:, None] == seeds[None, :]).astype(jnp.float32)
    seeded = (node_scores.astype(jnp.float32) + SEED_GAIN * hit).astype(jnp.bfloat16)
    blocks = seeded.reshape(NBLOCKS, BLK, Q)

    def gather_step(total, item):
        tiles, lists, scores = item
        terms = jnp.einsum('kij,iq->kjq', tiles.astype(jnp.float32), scores.astype(jnp.float32))
        return (total.at[lists].add(terms), None)
    sums, _ = lax.scan(gather_step, jnp.zeros((ABLOCKS, BLK, Q), jnp.float32), (node_tiles, node_lists, blocks))
    values = sums
    for step in range(ITERS):
        shared = values.astype(jnp.bfloat16)
        near = shared[anchor_lists]
        values = sums + jnp.einsum('akij,akjq->aiq', anchor_tiles.astype(jnp.float32), near.astype(jnp.float32))
    final_shared = values.astype(jnp.bfloat16)

    def back_step(carry, item):
        tiles, lists, scores = item
        back = jnp.einsum('kij,kjq->iq', tiles.astype(jnp.float32), final_shared[lists].astype(jnp.float32))
        resid = scores.astype(jnp.float32) - back
        energy = lax.optimization_barrier(jnp.mean(resid * resid, axis=1))
        return (carry, (resid * lax.rsqrt(energy + EPS)[:, None]).astype(jnp.bfloat16))
    _, ranked = lax.scan(back_step, jnp.zeros((), jnp.float32), (node_tiles, node_lists, blocks))
    return (ranked.reshape(NODES, Q), values.reshape(ANCHORS, Q))
```

```python
import functools

import jax
import jax.numpy as jnp
from jax import lax
from jax.experimental import pallas as pl
from jax.experimental.pallas import tpu as pltpu
from jax.sharding import PartitionSpec as P

ITERS = 2
SEED_GAIN = 4.0
EPS = 1e-05
B = 128
NB = 64
KN = 8
KA = 4
NA = 128
H = 2
R = B // H
STEP = 8
F32 = jnp.float32
BF16 = jnp.bfloat16
MESH = pl.DeviceIdType.MESH


def place(ids):
    z, y, core, slot = ids // 32, (ids // 8) % 4, (ids // 4) % 2, ids % 4
    first = z + core * (y - z)
    second = y + core * (z - y)
    return core * 64 + first * 16 + second * 4 + slot


def forward_kernel(places, seeds, scores, tiles, held, seeded, total):
    step = pl.program_id(0)
    start_row = lax.axis_index("node") * (NB * B)

    @pl.when(step == 0)
    def _():
        def clear(i, carry):
            total[i] = jnp.zeros((B, B), F32)
            return carry

        lax.fori_loop(0, NA, clear, 0, unroll=4)

    wanted = seeds[...]
    for b in range(STEP):
        first = start_row + (step * STEP + b) * B
        rows = lax.broadcasted_iota(jnp.int32, (B, B), 0) + first
        hit = (rows == wanted).astype(F32)
        block = scores[b * B : (b + 1) * B, :].astype(F32) + SEED_GAIN * hit
        flipped = block.T.astype(BF16)
        seeded[b] = flipped
        for k in range(KN):
            term = jnp.dot(flipped, tiles[b, k], preferred_element_type=F32)
            at = places[(step * STEP + b) * KN + k]
            total[at] += term

    @pl.when(step == pl.num_programs(0) - 1)
    def _():
        def narrow(i, carry):
            whole = total[i].astype(BF16)
            for h in range(H):
                held[h, i] = whole[h * R : (h + 1) * R]
            return carry

        lax.fori_loop(0, NA, narrow, 0, unroll=4)


def forward(places, seeds, scores, tiles):
    return pl.pallas_call(
        forward_kernel,
        grid_spec=pltpu.PrefetchScalarGridSpec(
            num_scalar_prefetch=1,
            grid=(NB // STEP,),
            in_specs=[
                pl.BlockSpec((1, B), lambda g, p: (0, 0)),
                pl.BlockSpec((STEP * B, B), lambda g, p: (g, 0)),
                pl.BlockSpec((STEP, KN, B, B), lambda g, p: (g, 0, 0, 0)),
            ],
            out_specs=[
                pl.BlockSpec((H, NA, R, B), lambda g, p: (0, 0, 0, 0)),
                pl.BlockSpec((STEP, B, B), lambda g, p: (g, 0, 0)),
            ],
            scratch_shapes=[pltpu.VMEM((NA, B, B), F32)],
        ),
        out_shape=[
            jax.ShapeDtypeStruct((H, NA, R, B), BF16),
            jax.ShapeDtypeStruct((NB, B, B), BF16),
        ],
        compiler_params=pltpu.CompilerParams(vmem_limit_bytes=40 << 20),
        cost_estimate=pl.CostEstimate(flops=2 * NB * KN * B**3, bytes_accessed=24 << 20, transcendentals=0),
        name="forward",
    )(places, seeds, scores, tiles)


CHUNKS = 4
PER = NB // CHUNKS
RS_SEMS = 4 + 6 + 6
AG_SEMS = 4 + 6 + 4
HALF_SEMS = RS_SEMS + (ITERS + 1) * AG_SEMS


def rest_kernel(places, near, held, seeded_in, atiles, tiles_in, rank_out, score_out, *scratch):
    scratch = list(scratch)
    take = lambda n: [scratch.pop(0) for _ in range(n)]
    tiles, seeded, resid, energy, others, ranked = take(6)
    own, mate = take(H), take(H)
    far, up, down, ra, rb, gm, gp = (take(H) for _ in range(7))
    far2, up2, down2, ra2, rb2, gm2, gp2 = (take(H) for _ in range(7))
    sums, values = take(H), take(H)
    shared = [take(H) for _ in range(ITERS + 1)]
    send_sems, recv_sems, local_sems, esend, erecv = take(5)

    node, pb = lax.axis_index("node"), lax.axis_index("pb")
    core = node % 2
    sf, ss = 8 - 6 * core, 2 + 6 * core
    pf, ps = (node // sf) % 4, (node // ss) % 4
    turn = lambda at, by: (at + by + 4) % 4
    f_up = node + (turn(pf, 1) - pf) * sf
    f_dn = node + (turn(pf, -1) - pf) * sf
    s_up = node + (turn(ps, 1) - ps) * ss
    s_dn = node + (turn(ps, -1) - ps) * ss
    sib = node + 1 - 2 * core

    locals_ = []

    def local(src, dst):
        copy = pltpu.make_async_copy(src, dst, local_sems.at[len(locals_)])
        copy.start()
        locals_.append(copy)
        return copy

    own_copies = [local(held.at[h, pl.ds(core * 64, 64)], own[h]) for h in range(H)]
    seeded_copy = local(seeded_in, seeded)
    tile_copies = [local(tiles_in.at[pl.ds(i * PER, PER)], tiles.at[pl.ds(i * PER, PER)]) for i in range(CHUNKS)]

    barrier = pltpu.get_barrier_semaphore()
    for peer in (sib, f_up, f_dn, s_up, s_dn):
        pl.semaphore_signal(barrier, inc=1, device_id={"node": peer}, device_id_type=MESH)
    for by in (1, 2, 3):
        pl.semaphore_signal(barrier, inc=1, device_id={"pb": turn(pb, by)}, device_id_type=MESH)
    pl.semaphore_wait(barrier, 8)

    started = []
    count = [0] * H

    def send(h, src, dst, peer):
        i = h * HALF_SEMS + count[h]
        count[h] += 1
        copy = pltpu.make_async_remote_copy(
            src_ref=src, dst_ref=dst, send_sem=send_sems.at[i], recv_sem=recv_sems.at[i],
            device_id={"node": peer}, device_id_type=MESH,
        )
        copy.start()
        started.append(copy)
        return copy

    def add_blocks(n, dst, dst_at, *terms):
        def body(i, carry):
            for u in range(2):
                j = i * 2 + u
                acc = terms[0][0][terms[0][1] + j].astype(F32)
                for ref, at in terms[1:]:
                    acc = acc + ref[at + j].astype(F32)
                dst[dst_at + j] = acc.astype(dst.dtype)
            return carry

        lax.fori_loop(0, n // 2, body, 0)

    def reduce_scatter(h):
        o, m = own[h], mate[h]
        other = (1 - core) * 64
        got = {}
        for by in (2, 1, 3, 0):
            f = turn(ps, by)
            got[by] = send(h, held.at[h, pl.ds(other + f * 16, 16)], m.at[pl.ds(f * 16, 16)], sib)
        yield
        own_copies[h].wait()
        got[2].wait_recv()
        at = turn(pf, 2) * 16
        add_blocks(16, far[h], 0, (o, at), (m, at))
        a1 = send(h, far[h].at[pl.ds(0, 8)], ra[h], f_up)
        b1 = send(h, far[h].at[pl.ds(8, 8)], rb[h], f_dn)
        at_up, at_dn = turn(pf, 1) * 16, turn(pf, -1) * 16
        got[1].wait_recv()
        add_blocks(8, up[h], 8, (o, at_up + 8), (m, at_up + 8))
        mb = send(h, up[h].at[pl.ds(8, 8)], gm[h].at[pl.ds(8, 8)], f_up)
        got[3].wait_recv()
        add_blocks(8, down[h], 0, (o, at_dn), (m, at_dn))
        pa = send(h, down[h].at[pl.ds(0, 8)], gp[h].at[pl.ds(0, 8)], f_dn)
        yield
        a1.wait_recv()
        add_blocks(8, up[h], 0, (o, at_up), (m, at_up), (ra[h], 0))
        ma = send(h, up[h].at[pl.ds(0, 8)], gm[h].at[pl.ds(0, 8)], f_up)
        b1.wait_recv()
        add_blocks(8, down[h], 8, (o, at_dn + 8), (m, at_dn + 8), (rb[h], 0))
        pb_ = send(h, down[h].at[pl.ds(8, 8)], gp[h].at[pl.ds(8, 8)], f_dn)
        yield
        got[0].wait_recv()
        for copy in (mb, pa, ma, pb_):
            copy.wait_recv()
        mine = pf * 16

        def part(s, skip):
            at = s * 4 + skip
            return (o, mine + at), (m, mine + at), (gm[h], at), (gp[h], at)

        s_far, s_a, s_b = turn(ps, 2), turn(ps, 1), turn(ps, -1)
        add_blocks(4, far2[h], 0, *part(s_far, 0))
        a1 = send(h, far2[h].at[pl.ds(0, 2)], ra2[h], s_up)
        b1 = send(h, far2[h].at[pl.ds(2, 2)], rb2[h], s_dn)
        add_blocks(2, up2[h], 2, *part(s_a, 2))
        mb = send(h, up2[h].at[pl.ds(2, 2)], gm2[h].at[pl.ds(2, 2)], s_up)
        add_blocks(2, down2[h], 0, *part(s_b, 0))
        pa = send(h, down2[h].at[pl.ds(0, 2)], gp2[h].at[pl.ds(0, 2)], s_dn)
        yield
        a1.wait_recv()
        add_blocks(2, up2[h], 0, *part(s_a, 0), (ra2[h], 0))
        ma = send(h, up2[h].at[pl.ds(0, 2)], gm2[h].at[pl.ds(0, 2)], s_up)
        b1.wait_recv()
        add_blocks(2, down2[h], 2, *part(s_b, 2), (rb2[h], 0))
        pb_ = send(h, down2[h].at[pl.ds(2, 2)], gp2[h].at[pl.ds(2, 2)], s_dn)
        yield
        for copy in (mb, pa, ma, pb_):
            copy.wait_recv()
        add_blocks(4, sums[h], 0, *part(ps, 0), (gm2[h], 0), (gp2[h], 0))

    def all_gather(h, buf):
        row = core * 64 + pf * 16
        mine = row + ps * 4
        at = lambda start, n: buf.at[pl.ds(start, n)]
        go = lambda start, n, peer: send(h, at(start, n), at(start, n), peer)
        u1 = go(mine, 4, s_up)
        d1 = go(mine, 4, s_dn)
        yield
        u1.wait_recv()
        u2 = go(row + turn(ps, -1) * 4, 2, s_up)
        d1.wait_recv()
        d2 = go(row + turn(ps, 1) * 4 + 2, 2, s_dn)
        yield
        u2.wait_recv()
        d2.wait_recv()
        ua = go(row, 8, f_up)
        db = go(row + 8, 8, f_dn)
        ub = go(row + 8, 8, f_up)
        da = go(row, 8, f_dn)
        across = [go(row, 16, sib)]
        yield
        base = core * 64
        low, high, far_ = base + turn(pf, -1) * 16, base + turn(pf, 1) * 16, base + turn(pf, 2) * 16
        ua.wait_recv()
        ua2 = go(low, 8, f_up)
        db.wait_recv()
        db2 = go(high + 8, 8, f_dn)
        yield
        ub.wait_recv()
        across.append(go(low, 16, sib))
        da.wait_recv()
        across.append(go(high, 16, sib))
        yield
        ua2.wait_recv()
        db2.wait_recv()
        across.append(go(far_, 16, sib))
        yield
        for copy in across:
            copy.wait_recv()

    def iterate(h, buf, out, keep):
        mine = core * 64 + pf * 16 + ps * 4
        for r in range(4):
            acc = sums[h][r]
            for k in range(0, KA, 2):
                left = jnp.concatenate([buf[near[r * KA + k + i]] for i in range(2)], axis=1)
                right = jnp.concatenate([atiles[r, k + i] for i in range(2)], axis=1)
                acc = acc + lax.dot_general(left, right, (((1,), (1,)), ((), ())), preferred_element_type=F32)
            if keep is not None:
                keep[r] = acc
            out[mine + r] = acc.astype(BF16)

    def pipeline(h):
        yield from reduce_scatter(h)
        mine = core * 64 + pf * 16 + ps * 4
        for r in range(4):
            shared[0][h][mine + r] = sums[h][r].astype(BF16)
        for t in range(ITERS):
            yield from all_gather(h, shared[t][h])
            iterate(h, shared[t][h], shared[t + 1][h], values[h] if t == ITERS - 1 else None)
        yield from all_gather(h, shared[ITERS][h])

    lines = [pipeline(h) for h in range(H)]
    live = list(range(H))
    next(lines[0])
    if H > 1:
        next(lines[1])
    while live:
        for h in list(live):
            try:
                next(lines[h])
            except StopIteration:
                live.remove(h)

    for r in range(4):
        whole = jnp.concatenate([values[h][r] for h in range(H)], axis=0)
        score_out[r * B : (r + 1) * B, :] = whole.T

    seeded_copy.wait()
    final = shared[ITERS]
    esends = []
    outs = []

    def finish(c):
        for copy in esends[c]:
            copy.wait_recv()

        def body(i, carry):
            for u in range(2):
                b = c * PER + i * 2 + u
                tot = energy[pl.ds(b, 1), :]
                for d in range(3):
                    tot = tot + others[d, pl.ds(b, 1), :]
                scale = lax.rsqrt(tot / 512.0 + EPS)
                block = (resid[b] * scale).astype(BF16)
                ranked[pl.ds(pl.multiple_of(b * B, B), B), :] = block.T
            return carry

        lax.fori_loop(0, PER // 2, body, 0)
        copy = pltpu.make_async_copy(
            ranked.at[pl.ds(c * PER * B, PER * B)], rank_out.at[pl.ds(c * PER * B, PER * B)],
            local_sems.at[H + 1 + CHUNKS + c],
        )
        copy.start()
        outs.append(copy)

    for c in range(CHUNKS):
        tile_copies[c].wait()

        def body(i, carry):
            for u in range(4):
                b = c * PER + i * 4 + u
                acc = None
                for k in range(0, KN, 2):
                    pieces = []
                    for j in range(2):
                        at = places[b * KN + k + j]
                        pieces.append(jnp.concatenate([final[h][at] for h in range(H)], axis=0))
                    left = jnp.concatenate(pieces, axis=1)
                    right = jnp.concatenate([tiles[b, k + j] for j in range(2)], axis=1)
                    part = lax.dot_general(left, right, (((1,), (1,)), ((), ())), preferred_element_type=F32)
                    acc = part if acc is None else acc + part
                res = seeded[b].astype(F32) - acc
                resid[b] = res
                energy[pl.ds(b, 1), :] = jnp.sum(res * res, axis=0, keepdims=True)
            return carry

        lax.fori_loop(0, PER // 4, body, 0)
        group = []
        for d in (1, 2, 3):
            i = c * 3 + d - 1
            copy = pltpu.make_async_remote_copy(
                src_ref=energy.at[pl.ds(c * PER, PER)], dst_ref=others.at[d - 1, pl.ds(c * PER, PER)],
                send_sem=esend.at[i], recv_sem=erecv.at[i],
                device_id={"pb": turn(pb, d)}, device_id_type=MESH,
            )
            copy.start()
            group.append(copy)
        esends.append(group)
        if c > 0:
            finish(c - 1)
    finish(CHUNKS - 1)

    for copy in started:
        copy.wait_send()
    for group in esends:
        for copy in group:
            copy.wait_send()
    for copy in outs:
        copy.wait()


def rest(places, near, held, seeded, atiles, tiles):
    vm = lambda *shape, dtype=BF16: pltpu.VMEM(shape, dtype)
    per_half = lambda n, dtype=BF16: [pltpu.VMEM((n, R, B), dtype) for _ in range(H)]
    scratch = [
        vm(NB, KN, B, B),
        vm(NB, B, B),
        vm(NB, B, B, dtype=F32),
        vm(NB, B, dtype=F32),
        vm(3, NB, B, dtype=F32),
        vm(NB * B, B),
    ]
    for n in (64, 64, 16, 16, 16, 8, 8, 16, 16, 4, 4, 4, 2, 2, 4, 4):
        scratch += per_half(n)
    scratch += per_half(4, F32) + per_half(4, F32)
    for _ in range(ITERS + 1):
        scratch += per_half(NA)
    sems = pltpu.SemaphoreType.DMA
    scratch += [
        sems((H * HALF_SEMS,)), sems((H * HALF_SEMS,)), sems((H + 1 + 2 * CHUNKS,)),
        sems((3 * CHUNKS,)), sems((3 * CHUNKS,)),
    ]
    smem = pl.BlockSpec(memory_space=pltpu.SMEM)
    vmem = pl.BlockSpec(memory_space=pltpu.VMEM)
    hbm = pl.BlockSpec(memory_space=pl.ANY)
    return pl.pallas_call(
        rest_kernel,
        in_specs=[smem, smem, hbm, hbm, vmem, hbm],
        out_specs=[hbm, vmem],
        out_shape=[jax.ShapeDtypeStruct((NB * B, B), BF16), jax.ShapeDtypeStruct((4 * B, B), F32)],
        scratch_shapes=scratch,
        compiler_params=pltpu.CompilerParams(
            collective_id=0, has_side_effects=True, vmem_limit_bytes=58 << 20
        ),
        cost_estimate=pl.CostEstimate(flops=2 * NB * KN * B**3, bytes_accessed=28 << 20, transcendentals=0),
        name="rest",
    )(places, near, held, seeded, atiles, tiles)


def shards(node_scores, seeds, node_lists, node_tiles, anchor_lists, anchor_tiles):
    places = place(node_lists).reshape(-1)
    own_lists = lax.dynamic_slice_in_dim(anchor_lists, lax.axis_index("node") * 4, 4, 0)
    near = place(own_lists).reshape(-1)
    held, seeded = forward(places, seeds.reshape(1, B), node_scores, node_tiles)
    ranking, anchor_scores = rest(places, near, held, seeded, anchor_tiles, node_tiles)
    return (ranking, anchor_scores)


def solution(mesh):
    in_specs = (
        P("node", "pb"),
        P("pb"),
        P("node", None),
        P("node", None, None, None),
        P(),
        P("node", None, None, None),
    )
    out_specs = (P("node", "pb"), P("node", "pb"))
    return jax.shard_map(shards, mesh=mesh, in_specs=in_specs, out_specs=out_specs, check_vma=False)
```

```python
import functools

import jax
import jax.numpy as jnp
from jax import lax
from jax.experimental import pallas as pl
from jax.experimental.pallas import tpu as pltpu
from jax.sharding import PartitionSpec as P

ITERS = 2
SEED_GAIN = 4.0
EPS = 1e-05
B = 128
NB = 64
KN = 8
KA = 4
NA = 128
H = 2
R = B // H
STEP = 8
FORWARD_VMEM, REST_VMEM = 56, 50
F32 = jnp.float32
BF16 = jnp.bfloat16
MESH = pl.DeviceIdType.MESH


def place(ids):
    z, y, core, slot = ids >> 5, (ids >> 3) & 3, (ids >> 2) & 1, ids & 3
    first = z + core * (y - z)
    second = y + core * (z - y)
    return (core << 6) + (first << 4) + (second << 2) + slot


def forward_kernel(lists, seeds, scores, tiles, held, seeded, total):
    step = pl.program_id(0)
    start_row = lax.axis_index("node") * (NB * B)

    @pl.when(step == 0)
    def _():
        def clear(i, carry):
            total[i] = jnp.zeros((B, B), F32)
            return carry

        lax.fori_loop(0, NA, clear, 0, unroll=4)

    wanted = seeds[...]
    for b in range(STEP):
        first = start_row + (step * STEP + b) * B
        rows = lax.broadcasted_iota(jnp.int32, (B, B), 0) + first
        hit = (rows == wanted).astype(F32)
        block = scores[b * B : (b + 1) * B, :].astype(F32) + SEED_GAIN * hit
        flipped = block.T.astype(BF16)
        seeded[b] = flipped
        for k in range(KN):
            term = jnp.dot(flipped, tiles[b, k], preferred_element_type=F32)
            at = place(lists[k, step * STEP + b])
            total[at] += term

    @pl.when(step == pl.num_programs(0) - 1)
    def _():
        def narrow(i, carry):
            whole = total[i].astype(BF16)
            for h in range(H):
                held[h, i] = whole[h * R : (h + 1) * R]
            return carry

        lax.fori_loop(0, NA, narrow, 0, unroll=4)


def forward(lists, seeds, scores, tiles):
    return pl.pallas_call(
        forward_kernel,
        grid_spec=pltpu.PrefetchScalarGridSpec(
            num_scalar_prefetch=1,
            grid=(NB // STEP,),
            in_specs=[
                pl.BlockSpec((1, B), lambda g, p: (0, 0)),
                pl.BlockSpec((STEP * B, B), lambda g, p: (g, 0)),
                pl.BlockSpec((STEP, KN, B, B), lambda g, p: (g, 0, 0, 0)),
            ],
            out_specs=[
                pl.BlockSpec((H, NA, R, B), lambda g, p: (0, 0, 0, 0)),
                pl.BlockSpec((STEP, B, B), lambda g, p: (g, 0, 0)),
            ],
            scratch_shapes=[pltpu.VMEM((NA, B, B), F32)],
        ),
        out_shape=[
            jax.ShapeDtypeStruct((H, NA, R, B), BF16),
            jax.ShapeDtypeStruct((NB, B, B), BF16),
        ],
        compiler_params=pltpu.CompilerParams(vmem_limit_bytes=FORWARD_VMEM << 20),
        cost_estimate=pl.CostEstimate(flops=2 * NB * KN * B**3, bytes_accessed=24 << 20, transcendentals=0),
        name="forward",
    )(lists, seeds, scores, tiles)


CHUNKS = 4
PER = NB // CHUNKS
RS_SEMS = 4 + 6 + 3
AG_SEMS = 3 + 6 + 4
HALF_SEMS = RS_SEMS + (ITERS + 1) * AG_SEMS
TILE_SEMS = 3 * 4


def rest_kernel(lists, near, held, seeded_in, atiles, tiles_in, rank_out, score_out, *scratch):
    scratch = list(scratch)
    take = lambda n: [scratch.pop(0) for _ in range(n)]
    tiles, seeded, resid, energy, others, ranked = take(6)
    own, mate = take(H), take(H)
    far, up, down, ra, rb, gm, gp = (take(H) for _ in range(7))
    out2, in2 = take(H), take(H)
    sums, values = take(H), take(H)
    (row_tiles,) = take(1)
    shared = [take(H) for _ in range(ITERS + 1)]
    send_sems, recv_sems, local_sems, esend, erecv = take(5)

    node, pb = lax.axis_index("node"), lax.axis_index("pb")
    core = node % 2
    sf, ss = 8 - 6 * core, 2 + 6 * core
    pf, ps = (node // sf) % 4, (node // ss) % 4
    turn = lambda at, by: (at + by + 4) % 4
    f_up = node + (turn(pf, 1) - pf) * sf
    f_dn = node + (turn(pf, -1) - pf) * sf
    s_up = node + (turn(ps, 1) - ps) * ss
    s_dn = node + (turn(ps, -1) - ps) * ss
    s_far = node + (turn(ps, 2) - ps) * ss
    ring = ((2, s_far), (1, s_up), (-1, s_dn))
    sib = node + 1 - 2 * core

    locals_ = []

    def local(src, dst):
        copy = pltpu.make_async_copy(src, dst, local_sems.at[len(locals_)])
        copy.start()
        locals_.append(copy)
        return copy

    own_copies = [local(held.at[h, pl.ds(core * 64, 64)], own[h]) for h in range(H)]
    own_tiles_copy = local(atiles, row_tiles.at[ps])
    seeded_copy = local(seeded_in, seeded)
    tile_copies = [local(tiles_in.at[pl.ds(i * PER, PER)], tiles.at[pl.ds(i * PER, PER)]) for i in range(CHUNKS)]

    barrier = pltpu.get_barrier_semaphore()
    for peer in (sib, f_up, f_dn, s_up, s_dn, s_far):
        pl.semaphore_signal(barrier, inc=1, device_id={"node": peer}, device_id_type=MESH)
    for by in (1, 2, 3):
        pl.semaphore_signal(barrier, inc=1, device_id={"pb": turn(pb, by)}, device_id_type=MESH)
    pl.semaphore_wait(barrier, 9)

    started = []
    count = [0] * (H + 1)

    def send(h, src, dst, peer):
        i = h * HALF_SEMS + count[h]
        count[h] += 1
        copy = pltpu.make_async_remote_copy(
            src_ref=src, dst_ref=dst, send_sem=send_sems.at[i], recv_sem=recv_sems.at[i],
            device_id={"node": peer}, device_id_type=MESH,
        )
        copy.start()
        started.append(copy)
        return copy

    tile_sends = []

    def share_tiles(n):
        for _ in range(n):
            i = len(tile_sends)
            if i < 12:
                r, (_, peer) = i // 3, ring[i % 3]
                tile_sends.append(send(H, atiles.at[r], row_tiles.at[ps, r], peer))

    def add_blocks(n, dst, dst_at, *terms):
        def body(i, carry):
            for u in range(2):
                j = i * 2 + u
                acc = terms[0][0][terms[0][1] + j].astype(F32)
                for ref, at in terms[1:]:
                    acc = acc + ref[at + j].astype(F32)
                dst[dst_at + j] = acc.astype(dst.dtype)
            return carry

        lax.fori_loop(0, n // 2, body, 0)

    def reduce_scatter(h):
        o, m = own[h], mate[h]
        other = (1 - core) * 64
        got = {}
        for by in (2, 1, 3, 0):
            f = turn(ps, by)
            got[by] = send(h, held.at[h, pl.ds(other + f * 16, 16)], m.at[pl.ds(f * 16, 16)], sib)
        yield
        own_copies[h].wait()
        got[2].wait_recv()
        at = turn(pf, 2) * 16
        add_blocks(16, far[h], 0, (o, at), (m, at))
        a1 = send(h, far[h].at[pl.ds(0, 8)], ra[h], f_up)
        b1 = send(h, far[h].at[pl.ds(8, 8)], rb[h], f_dn)
        at_up, at_dn = turn(pf, 1) * 16, turn(pf, -1) * 16
        got[1].wait_recv()
        add_blocks(8, up[h], 8, (o, at_up + 8), (m, at_up + 8))
        mb = send(h, up[h].at[pl.ds(8, 8)], gm[h].at[pl.ds(8, 8)], f_up)
        got[3].wait_recv()
        add_blocks(8, down[h], 0, (o, at_dn), (m, at_dn))
        pa = send(h, down[h].at[pl.ds(0, 8)], gp[h].at[pl.ds(0, 8)], f_dn)
        yield
        a1.wait_recv()
        add_blocks(8, up[h], 0, (o, at_up), (m, at_up), (ra[h], 0))
        ma = send(h, up[h].at[pl.ds(0, 8)], gm[h].at[pl.ds(0, 8)], f_up)
        b1.wait_recv()
        add_blocks(8, down[h], 8, (o, at_dn + 8), (m, at_dn + 8), (rb[h], 0))
        pb_ = send(h, down[h].at[pl.ds(8, 8)], gp[h].at[pl.ds(8, 8)], f_dn)
        yield
        got[0].wait_recv()
        for copy in (mb, pa, ma, pb_):
            copy.wait_recv()
        mine = pf * 16

        def part(s, skip):
            at = s * 4 + skip
            return (o, mine + at), (m, mine + at), (gm[h], at), (gp[h], at)

        hops = []
        for by, peer in ring:
            to = turn(ps, by) * 4
            add_blocks(4, out2[h], to, *part(turn(ps, by), 0))
            hops.append(send(h, out2[h].at[pl.ds(to, 4)], in2[h].at[ps], peer))
        share_tiles(3)
        yield
        add_blocks(4, sums[h], ps * 4, *part(ps, 0))
        for copy in hops:
            copy.wait_recv()
        for by in (2, 1, 3):
            add_blocks(4, sums[h], ps * 4, (sums[h], ps * 4), (in2[h].at[turn(ps, by)], 0))

    def all_gather(h, buf, whole):
        base = core * 64
        row = base + pf * 16
        mine = row + ps * 4
        at = lambda start, n: buf.at[pl.ds(start, n)]
        go = lambda start, n, peer: send(h, at(start, n), at(start, n), peer)
        if not whole:
            hops = [go(mine, 4, peer) for _, peer in ring]
            share_tiles(3)
            yield
            for copy in hops:
                copy.wait_recv()
        ua = go(row, 8, f_up)
        db = go(row + 8, 8, f_dn)
        ub = go(row + 8, 8, f_up)
        da = go(row, 8, f_dn)
        across = [go(row, 16, sib)]
        yield
        low, high, far_ = base + turn(pf, -1) * 16, base + turn(pf, 1) * 16, base + turn(pf, 2) * 16
        ua.wait_recv()
        ua2 = go(low, 8, f_up)
        db.wait_recv()
        db2 = go(high + 8, 8, f_dn)
        ub.wait_recv()
        across.append(go(low, 16, sib))
        da.wait_recv()
        across.append(go(high, 16, sib))
        yield
        ua2.wait_recv()
        db2.wait_recv()
        across.append(go(far_, 16, sib))
        yield
        for copy in across:
            copy.wait_recv()

    def iterate(h, buf, out):
        row = core * 64 + pf * 16

        def body(s, carry):
            anchors = (node + (s - ps) * ss) * 4
            for r in range(4):
                acc = sums[h][s * 4 + r]
                for k in range(0, KA, 2):
                    left = jnp.concatenate([buf[place(near[k + i, anchors + r])] for i in range(2)], axis=1)
                    right = jnp.concatenate([row_tiles[s, r, k + i] for i in range(2)], axis=1)
                    acc = acc + lax.dot_general(left, right, (((1,), (1,)), ((), ())), preferred_element_type=F32)
                values[h][s * 4 + r] = acc
                out[row + s * 4 + r] = acc.astype(BF16)
            return carry

        lax.fori_loop(0, 4, body, 0)

    def pipeline(h):
        yield from reduce_scatter(h)
        row = core * 64 + pf * 16
        add_blocks(4, shared[0][h], row + ps * 4, (sums[h], ps * 4))
        yield from all_gather(h, shared[0][h], False)
        for by, _ in ring:
            at = turn(ps, by) * 4
            add_blocks(4, sums[h], at, (shared[0][h], row + at))
        if h == 0:
            for copy in tile_sends:
                copy.wait_recv()
            own_tiles_copy.wait()
        for t in range(ITERS):
            iterate(h, shared[t][h], shared[t + 1][h])
            yield from all_gather(h, shared[t + 1][h], True)

    lines = [pipeline(h) for h in range(H)]
    live = list(range(H))
    next(lines[0])
    if H > 1:
        next(lines[1])
    while live:
        for h in list(live):
            try:
                next(lines[h])
            except StopIteration:
                live.remove(h)

    for r in range(4):
        whole = jnp.concatenate([values[h][ps * 4 + r] for h in range(H)], axis=0)
        score_out[r * B : (r + 1) * B, :] = whole.T

    seeded_copy.wait()
    final = shared[ITERS]
    esends = []
    outs = []

    def finish(c):
        for copy in esends[c]:
            copy.wait_recv()

        def body(i, carry):
            for u in range(2):
                b = c * PER + i * 2 + u
                tot = energy[pl.ds(b, 1), :]
                for d in range(3):
                    tot = tot + others[d, pl.ds(b, 1), :]
                scale = lax.rsqrt(tot / 512.0 + EPS)
                block = (resid[b] * scale).astype(BF16)
                ranked[pl.ds(pl.multiple_of(b * B, B), B), :] = block.T
            return carry

        lax.fori_loop(0, PER // 2, body, 0)
        copy = pltpu.make_async_copy(
            ranked.at[pl.ds(c * PER * B, PER * B)], rank_out.at[pl.ds(c * PER * B, PER * B)],
            local_sems.at[H + 2 + CHUNKS + c],
        )
        copy.start()
        outs.append(copy)

    for c in range(CHUNKS):
        tile_copies[c].wait()

        def body(i, carry):
            for u in range(4):
                b = c * PER + i * 4 + u
                acc = None
                for k in range(0, KN, 2):
                    pieces = []
                    for j in range(2):
                        at = place(lists[k + j, b])
                        pieces.append(jnp.concatenate([final[h][at] for h in range(H)], axis=0))
                    left = jnp.concatenate(pieces, axis=1)
                    right = jnp.concatenate([tiles[b, k + j] for j in range(2)], axis=1)
                    part = lax.dot_general(left, right, (((1,), (1,)), ((), ())), preferred_element_type=F32)
                    acc = part if acc is None else acc + part
                res = seeded[b].astype(F32) - acc
                resid[b] = res
                energy[pl.ds(b, 1), :] = jnp.sum(res * res, axis=0, keepdims=True)
            return carry

        lax.fori_loop(0, PER // 4, body, 0)
        group = []
        for d in (1, 2, 3):
            i = c * 3 + d - 1
            copy = pltpu.make_async_remote_copy(
                src_ref=energy.at[pl.ds(c * PER, PER)], dst_ref=others.at[d - 1, pl.ds(c * PER, PER)],
                send_sem=esend.at[i], recv_sem=erecv.at[i],
                device_id={"pb": turn(pb, d)}, device_id_type=MESH,
            )
            copy.start()
            group.append(copy)
        esends.append(group)
        if c > 0:
            finish(c - 1)
    finish(CHUNKS - 1)

    for copy in started:
        copy.wait_send()
    for group in esends:
        for copy in group:
            copy.wait_send()
    for copy in outs:
        copy.wait()


def rest(lists, near, held, seeded, atiles, tiles):
    vm = lambda *shape, dtype=BF16: pltpu.VMEM(shape, dtype)
    per_half = lambda n, dtype=BF16: [pltpu.VMEM((n, R, B), dtype) for _ in range(H)]
    scratch = [
        vm(NB, KN, B, B),
        vm(NB, B, B),
        vm(NB, B, B, dtype=F32),
        vm(NB, B, dtype=F32),
        vm(3, NB, B, dtype=F32),
        vm(NB * B, B),
    ]
    for n in (64, 64, 16, 16, 16, 8, 8, 16, 16, 16):
        scratch += per_half(n)
    scratch += [vm(4, 4, R, B) for _ in range(H)]
    scratch += per_half(16, F32) + per_half(16, F32)
    scratch += [vm(4, 4, KA, B, B)]
    for _ in range(ITERS + 1):
        scratch += per_half(NA)
    sems = pltpu.SemaphoreType.DMA
    scratch += [
        sems((H * HALF_SEMS + TILE_SEMS,)), sems((H * HALF_SEMS + TILE_SEMS,)), sems((H + 2 + 2 * CHUNKS,)),
        sems((3 * CHUNKS,)), sems((3 * CHUNKS,)),
    ]
    smem = pl.BlockSpec(memory_space=pltpu.SMEM)
    vmem = pl.BlockSpec(memory_space=pltpu.VMEM)
    hbm = pl.BlockSpec(memory_space=pl.ANY)
    return pl.pallas_call(
        rest_kernel,
        in_specs=[smem, smem, hbm, hbm, hbm, hbm],
        out_specs=[hbm, vmem],
        out_shape=[jax.ShapeDtypeStruct((NB * B, B), BF16), jax.ShapeDtypeStruct((4 * B, B), F32)],
        scratch_shapes=scratch,
        compiler_params=pltpu.CompilerParams(
            collective_id=0, has_side_effects=True, vmem_limit_bytes=REST_VMEM << 20
        ),
        cost_estimate=pl.CostEstimate(flops=2 * NB * KN * B**3, bytes_accessed=28 << 20, transcendentals=0),
        name="rest",
    )(lists, near, held, seeded, atiles, tiles)


def shards(node_scores, seeds, node_lists, node_tiles, anchor_lists, anchor_tiles):
    lists = node_lists.T
    held, seeded = forward(lists, seeds.reshape(1, B), node_scores, node_tiles)
    ranking, anchor_scores = rest(lists, anchor_lists.T, held, seeded, anchor_tiles, node_tiles)
    return (ranking, anchor_scores)


def solution(mesh):
    in_specs = (
        P("node", "pb"),
        P("pb"),
        P("node", None),
        P("node", None, None, None),
        P(),
        P("node", None, None, None),
    )
    out_specs = (P("node", "pb"), P("node", "pb"))
    return jax.shard_map(shards, mesh=mesh, in_specs=in_specs, out_specs=out_specs, check_vma=False)
```

```python
import functools

import jax
import jax.numpy as jnp
from jax import lax
from jax.experimental import pallas as pl
from jax.experimental.pallas import tpu as pltpu
from jax.sharding import PartitionSpec as P

ITERS = 2
SEED_GAIN = 4.0
EPS = 1e-05
B = 128
NB = 64
KN = 8
KA = 4
NA = 128
H = 2
R = B // H
PIECES = 4
STEP = 8
FORWARD_VMEM, REST_VMEM = 56, 50
F32 = jnp.float32
BF16 = jnp.bfloat16
MESH = pl.DeviceIdType.MESH


def place(ids):
    z, y, core, slot = ids >> 5, (ids >> 3) & 3, (ids >> 2) & 1, ids & 3
    first = z + core * (y - z)
    second = y + core * (z - y)
    return (core << 6) + (first << 4) + (second << 2) + slot


def forward_kernel(
    lists, seeds, scores_in, tiles_in, held, seeded_out,
    total, narrow, tiles, scores, seeded, out_sems, tile_sems, score_sems, seeded_sems,
):
    start_row = lax.axis_index("node") * (NB * B)
    rows_of = lambda g: pl.ds(pl.multiple_of(g * (STEP * B), STEP * B), STEP * B)
    blocks_of = lambda g: pl.ds(g * STEP, STEP)
    score_copy = lambda g: pltpu.make_async_copy(scores_in.at[rows_of(g)], scores.at[rows_of(g)], score_sems.at[g])
    tile_copy = lambda g: pltpu.make_async_copy(tiles_in.at[blocks_of(g)], tiles.at[blocks_of(g)], tile_sems.at[g])
    seeded_copy = lambda g: pltpu.make_async_copy(seeded.at[blocks_of(g)], seeded_out.at[blocks_of(g)], seeded_sems.at[g])
    for g in range(NB // STEP):
        score_copy(g).start()
        tile_copy(g).start()

    def clear(i, carry):
        for u in range(4):
            total[i * 4 + u] = jnp.zeros((B, B), F32)
        return carry

    lax.fori_loop(0, NA // 4, clear, 0)
    wanted = seeds[...]

    def group(g, carry):
        score_copy(g).wait()
        tile_copy(g).wait()
        for u in range(STEP):
            b = g * STEP + u
            at_rows = pl.ds(pl.multiple_of(b * B, B), B)
            rows = lax.broadcasted_iota(jnp.int32, (B, B), 0) + (start_row + b * B)
            hit = (rows == wanted).astype(F32)
            block = scores[at_rows, :].astype(F32) + SEED_GAIN * hit
            flipped = block.astype(BF16).T
            seeded[b] = flipped
            for k in range(KN):
                term = jnp.dot(flipped, tiles[b, k], preferred_element_type=F32)
                total[place(lists[k, b])] += term
        seeded_copy(g).start()
        return carry

    lax.fori_loop(0, NB // STEP, group, 0)
    copies = []
    for c in range(PIECES):

        def body(i, carry):
            for u in range(4):
                a = c * (NA // PIECES) + i * 4 + u
                whole = total[a].astype(BF16)
                for h in range(H):
                    narrow[h, a] = whole[h * R : (h + 1) * R]
            return carry

        lax.fori_loop(0, NA // PIECES // 4, body, 0)
        at = pl.ds(c * (NA // PIECES), NA // PIECES)
        for h in range(H):
            copy = pltpu.make_async_copy(narrow.at[h, at], held.at[h, at], out_sems.at[c * H + h])
            copy.start()
            copies.append(copy)
    for copy in copies:
        copy.wait()
    for g in range(NB // STEP):
        seeded_copy(g).wait()


def forward(lists, seeds, scores, tiles):
    hbm = pl.BlockSpec(memory_space=pl.ANY)
    sems = pltpu.SemaphoreType.DMA
    return pl.pallas_call(
        forward_kernel,
        in_specs=[pl.BlockSpec(memory_space=pltpu.SMEM), pl.BlockSpec(memory_space=pltpu.VMEM), hbm, hbm],
        out_specs=[hbm, hbm],
        out_shape=[
            jax.ShapeDtypeStruct((H, NA, R, B), BF16),
            jax.ShapeDtypeStruct((NB, B, B), BF16),
        ],
        scratch_shapes=[
            pltpu.VMEM((NA, B, B), F32),
            pltpu.VMEM((H, NA, R, B), BF16),
            pltpu.VMEM((NB, KN, B, B), BF16),
            pltpu.VMEM((NB * B, B), BF16),
            pltpu.VMEM((NB, B, B), BF16),
            sems((PIECES * H,)),
            sems((NB // STEP,)),
            sems((NB // STEP,)),
            sems((NB // STEP,)),
        ],
        compiler_params=pltpu.CompilerParams(vmem_limit_bytes=FORWARD_VMEM << 20),
        cost_estimate=pl.CostEstimate(flops=2 * NB * KN * B**3, bytes_accessed=24 << 20, transcendentals=0),
        name="forward",
    )(lists, seeds, scores, tiles)


CHUNKS = 4
PER = NB // CHUNKS
UNROLL = 8
RS_SEMS = 4 + 6 + 3
AG_SEMS = 3 + 6 + 4
HALF_SEMS = RS_SEMS + (ITERS + 1) * AG_SEMS
TILE_SEMS = 3 * 4


def rest_kernel(lists, near, held, seeded_in, atiles, tiles_in, rank_out, score_out, *scratch):
    scratch = list(scratch)
    take = lambda n: [scratch.pop(0) for _ in range(n)]
    tiles, seeded, resid, energy, others = take(5)
    own, mate = take(H), take(H)
    far, up, down, ra, rb, gm, gp = (take(H) for _ in range(7))
    out2, in2 = take(H), take(H)
    sums, values = take(H), take(H)
    (row_tiles,) = take(1)
    shared = [take(H) for _ in range(ITERS + 1)]
    send_sems, recv_sems, local_sems, esend, erecv = take(5)

    node, pb = lax.axis_index("node"), lax.axis_index("pb")
    core = node % 2
    sf, ss = 8 - 6 * core, 2 + 6 * core
    pf, ps = (node // sf) % 4, (node // ss) % 4
    turn = lambda at, by: (at + by + 4) % 4
    f_up = node + (turn(pf, 1) - pf) * sf
    f_dn = node + (turn(pf, -1) - pf) * sf
    s_up = node + (turn(ps, 1) - ps) * ss
    s_dn = node + (turn(ps, -1) - ps) * ss
    s_far = node + (turn(ps, 2) - ps) * ss
    ring = ((2, s_far), (1, s_up), (-1, s_dn))
    sib = node + 1 - 2 * core

    locals_ = []

    def local(src, dst):
        copy = pltpu.make_async_copy(src, dst, local_sems.at[len(locals_)])
        copy.start()
        locals_.append(copy)
        return copy

    own_copies = [local(held.at[h, pl.ds(core * 64, 64)], own[h]) for h in range(H)]
    own_tiles_copy = local(atiles, row_tiles.at[ps])
    seeded_copy = local(seeded_in, seeded)
    load_tiles = lambda: [
        local(tiles_in.at[pl.ds(i * PER, PER)], tiles.at[pl.ds(i * PER, PER)]) for i in range(CHUNKS)
    ]

    barrier = pltpu.get_barrier_semaphore()
    for peer in (sib, f_up, f_dn, s_up, s_dn, s_far):
        pl.semaphore_signal(barrier, inc=1, device_id={"node": peer}, device_id_type=MESH)
    for by in (1, 2, 3):
        pl.semaphore_signal(barrier, inc=1, device_id={"pb": turn(pb, by)}, device_id_type=MESH)
    pl.semaphore_wait(barrier, 9)

    started = []
    count = [0] * (H + 1)

    def send(h, src, dst, peer):
        i = h * HALF_SEMS + count[h]
        count[h] += 1
        copy = pltpu.make_async_remote_copy(
            src_ref=src, dst_ref=dst, send_sem=send_sems.at[i], recv_sem=recv_sems.at[i],
            device_id=peer if isinstance(peer, dict) else {"node": peer}, device_id_type=MESH,
        )
        copy.start()
        started.append(copy)
        return copy

    def pass_tiles_on():
        for copy in tile_hops:
            copy.wait_recv()
        return [
            send(H, row_tiles.at[turn(ps, by), pb], row_tiles.at[turn(ps, by), pb], {"pb": turn(pb, d)})
            for by, _ in ring for d in (1, 2, 3)
        ]

    def add_blocks(n, dst, dst_at, *terms):
        def body(i, carry):
            for u in range(4):
                j = i * 4 + u
                acc = terms[0][0][terms[0][1] + j].astype(F32)
                for ref, at in terms[1:]:
                    acc = acc + ref[at + j].astype(F32)
                dst[dst_at + j] = acc.astype(dst.dtype)
            return carry

        lax.fori_loop(0, n // 4, body, 0)

    def reduce_scatter(h):
        o, m = own[h], mate[h]
        other = (1 - core) * 64
        got = {}
        for by in (2, 1, 3, 0):
            f = turn(ps, by)
            got[by] = send(h, held.at[h, pl.ds(other + f * 16, 16)], m.at[pl.ds(f * 16, 16)], sib)
        yield
        own_copies[h].wait()
        got[2].wait_recv()
        at = turn(pf, 2) * 16
        add_blocks(16, far[h], 0, (o, at), (m, at))
        a1 = send(h, far[h].at[pl.ds(0, 8)], ra[h], f_up)
        b1 = send(h, far[h].at[pl.ds(8, 8)], rb[h], f_dn)
        at_up, at_dn = turn(pf, 1) * 16, turn(pf, -1) * 16
        got[1].wait_recv()
        add_blocks(8, up[h], 8, (o, at_up + 8), (m, at_up + 8))
        mb = send(h, up[h].at[pl.ds(8, 8)], gm[h].at[pl.ds(8, 8)], f_up)
        got[3].wait_recv()
        add_blocks(8, down[h], 0, (o, at_dn), (m, at_dn))
        pa = send(h, down[h].at[pl.ds(0, 8)], gp[h].at[pl.ds(0, 8)], f_dn)
        yield
        a1.wait_recv()
        add_blocks(8, up[h], 0, (o, at_up), (m, at_up), (ra[h], 0))
        ma = send(h, up[h].at[pl.ds(0, 8)], gm[h].at[pl.ds(0, 8)], f_up)
        b1.wait_recv()
        add_blocks(8, down[h], 8, (o, at_dn + 8), (m, at_dn + 8), (rb[h], 0))
        pb_ = send(h, down[h].at[pl.ds(8, 8)], gp[h].at[pl.ds(8, 8)], f_dn)
        yield
        got[0].wait_recv()
        for copy in (mb, pa, ma, pb_):
            copy.wait_recv()
        mine = pf * 16

        def part(s, skip):
            at = s * 4 + skip
            return (o, mine + at), (m, mine + at), (gm[h], at), (gp[h], at)

        hops = []
        for by, peer in ring:
            to = turn(ps, by) * 4
            add_blocks(4, out2[h], to, *part(turn(ps, by), 0))
            hops.append(send(h, out2[h].at[pl.ds(to, 4)], in2[h].at[ps], peer))
        yield
        add_blocks(4, sums[h], ps * 4, *part(ps, 0))
        for copy in hops:
            copy.wait_recv()
        for by in (2, 1, 3):
            add_blocks(4, sums[h], ps * 4, (sums[h], ps * 4), (in2[h].at[turn(ps, by)], 0))

    def all_gather(h, buf, whole):
        base = core * 64
        row = base + pf * 16
        mine = row + ps * 4
        at = lambda start, n: buf.at[pl.ds(start, n)]
        go = lambda start, n, peer: send(h, at(start, n), at(start, n), peer)
        if not whole:
            hops = [go(mine, 4, peer) for _, peer in ring]
            yield
            for copy in hops:
                copy.wait_recv()
        ua = go(row, 8, f_up)
        db = go(row + 8, 8, f_dn)
        ub = go(row + 8, 8, f_up)
        da = go(row, 8, f_dn)
        across = [go(row, 16, sib)]
        yield
        low, high, far_ = base + turn(pf, -1) * 16, base + turn(pf, 1) * 16, base + turn(pf, 2) * 16
        ua.wait_recv()
        ua2 = go(low, 8, f_up)
        db.wait_recv()
        db2 = go(high + 8, 8, f_dn)
        ub.wait_recv()
        across.append(go(low, 16, sib))
        da.wait_recv()
        across.append(go(high, 16, sib))
        yield
        ua2.wait_recv()
        db2.wait_recv()
        across.append(go(far_, 16, sib))
        yield
        for copy in across:
            copy.wait_recv()

    def iterate(h, buf, out):
        row = core * 64 + pf * 16

        def body(s, carry):
            anchors = (node + (s - ps) * ss) * 4
            for r in range(4):
                acc = sums[h][s * 4 + r]
                for k in range(0, KA, 2):
                    left = jnp.concatenate([buf[place(near[k + i, anchors + r])] for i in range(2)], axis=1)
                    right = jnp.concatenate([row_tiles[s, r, k + i] for i in range(2)], axis=1)
                    acc = acc + lax.dot_general(left, right, (((1,), (1,)), ((), ())), preferred_element_type=F32)
                values[h][s * 4 + r] = acc
                out[row + s * 4 + r] = acc.astype(BF16)
            return carry

        lax.fori_loop(0, 4, body, 0)

    def pipeline(h):
        yield from reduce_scatter(h)
        row = core * 64 + pf * 16
        add_blocks(4, shared[0][h], row + ps * 4, (sums[h], ps * 4))
        yield from all_gather(h, shared[0][h], False)
        for by, _ in ring:
            at = turn(ps, by) * 4
            add_blocks(4, sums[h], at, (shared[0][h], row + at))
        if h == 0:
            for copy in tile_passes:
                copy.wait_recv()
            own_tiles_copy.wait()
        for t in range(ITERS):
            iterate(h, shared[t][h], shared[t + 1][h])
            yield from all_gather(h, shared[t + 1][h], True)

    lines = [pipeline(h) for h in range(H)]
    live = list(range(H))
    for line in lines:
        next(line)
    tile_hops = [send(H, atiles.at[pb], row_tiles.at[ps, pb], peer) for _, peer in ring]
    for line in lines:
        next(line)
    tile_passes = pass_tiles_on()
    tile_copies = load_tiles()
    while live:
        for h in list(live):
            try:
                next(lines[h])
            except StopIteration:
                live.remove(h)

    for r in range(4):
        whole = jnp.concatenate([values[h][ps * 4 + r] for h in range(H)], axis=0)
        score_out[r * B : (r + 1) * B, :] = whole.T

    seeded_copy.wait()
    final = shared[ITERS]
    esends = []

    def finish(c):
        for copy in esends[c]:
            copy.wait_recv()

        def body(i, carry):
            for u in range(UNROLL):
                b = c * PER + i * UNROLL + u
                tot = energy[pl.ds(b, 1), :]
                for d in range(3):
                    tot = tot + others[d, pl.ds(b, 1), :]
                scale = lax.rsqrt(tot / 512.0 + EPS)
                block = (resid[b] * scale).astype(BF16)
                rank_out[pl.ds(pl.multiple_of(b * B, B), B), :] = block.T
            return carry

        lax.fori_loop(0, PER // UNROLL, body, 0)

    for c in range(CHUNKS):
        tile_copies[c].wait()

        def body(i, carry):
            for u in range(UNROLL):
                b = c * PER + i * UNROLL + u
                acc = None
                for k in range(0, KN, 2):
                    pieces = []
                    for j in range(2):
                        at = place(lists[k + j, b])
                        pieces.append(jnp.concatenate([final[h][at] for h in range(H)], axis=0))
                    left = jnp.concatenate(pieces, axis=1)
                    right = jnp.concatenate([tiles[b, k + j] for j in range(2)], axis=1)
                    part = lax.dot_general(left, right, (((1,), (1,)), ((), ())), preferred_element_type=F32)
                    acc = part if acc is None else acc + part
                res = seeded[b].astype(F32) - acc
                resid[b] = res
                energy[pl.ds(b, 1), :] = jnp.sum(res * res, axis=0, keepdims=True)
            return carry

        lax.fori_loop(0, PER // UNROLL, body, 0)
        group = []
        for d in (1, 2, 3):
            i = c * 3 + d - 1
            copy = pltpu.make_async_remote_copy(
                src_ref=energy.at[pl.ds(c * PER, PER)], dst_ref=others.at[d - 1, pl.ds(c * PER, PER)],
                send_sem=esend.at[i], recv_sem=erecv.at[i],
                device_id={"pb": turn(pb, d)}, device_id_type=MESH,
            )
            copy.start()
            group.append(copy)
        esends.append(group)
    for c in range(CHUNKS):
        finish(c)

    for copy in started:
        copy.wait_send()
    for group in esends:
        for copy in group:
            copy.wait_send()


def rest(lists, near, held, seeded, atiles, tiles):
    vm = lambda *shape, dtype=BF16: pltpu.VMEM(shape, dtype)
    per_half = lambda n, dtype=BF16: [pltpu.VMEM((n, R, B), dtype) for _ in range(H)]
    scratch = [
        vm(NB, KN, B, B),
        vm(NB, B, B),
        vm(NB, B, B, dtype=F32),
        vm(NB, B, dtype=F32),
        vm(3, NB, B, dtype=F32),
    ]
    for n in (64, 64, 16, 16, 16, 8, 8, 16, 16, 16):
        scratch += per_half(n)
    scratch += [vm(4, 4, R, B) for _ in range(H)]
    scratch += per_half(16, F32) + per_half(16, F32)
    scratch += [vm(4, 4, KA, B, B)]
    for _ in range(ITERS + 1):
        scratch += per_half(NA)
    sems = pltpu.SemaphoreType.DMA
    scratch += [
        sems((H * HALF_SEMS + TILE_SEMS,)), sems((H * HALF_SEMS + TILE_SEMS,)), sems((H + 2 + CHUNKS,)),
        sems((3 * CHUNKS,)), sems((3 * CHUNKS,)),
    ]
    smem = pl.BlockSpec(memory_space=pltpu.SMEM)
    vmem = pl.BlockSpec(memory_space=pltpu.VMEM)
    hbm = pl.BlockSpec(memory_space=pl.ANY)
    return pl.pallas_call(
        rest_kernel,
        in_specs=[smem, smem, hbm, hbm, hbm, hbm],
        out_specs=[vmem, vmem],
        out_shape=[jax.ShapeDtypeStruct((NB * B, B), BF16), jax.ShapeDtypeStruct((4 * B, B), F32)],
        scratch_shapes=scratch,
        compiler_params=pltpu.CompilerParams(
            collective_id=0, has_side_effects=True, vmem_limit_bytes=REST_VMEM << 20
        ),
        cost_estimate=pl.CostEstimate(flops=2 * NB * KN * B**3, bytes_accessed=28 << 20, transcendentals=0),
        name="rest",
    )(lists, near, held, seeded, atiles, tiles)


def shards(node_scores, seeds, node_lists, node_tiles, anchor_lists, anchor_tiles):
    lists = node_lists.T
    held, seeded = forward(lists, seeds.reshape(1, B), node_scores, node_tiles)
    ranking, anchor_scores = rest(lists, anchor_lists.T, held, seeded, anchor_tiles, node_tiles)
    return (ranking, anchor_scores)


def solution(mesh):
    in_specs = (
        P("node", "pb"),
        P("pb"),
        P("node", None),
        P("node", None, None, None),
        P(),
        P("node", None, None, None),
    )
    out_specs = (P("node", "pb"), P("node", "pb"))
    return jax.shard_map(shards, mesh=mesh, in_specs=in_specs, out_specs=out_specs, check_vma=False)
```

```python
import functools

import jax
import jax.numpy as jnp
from jax import lax
from jax.experimental import pallas as pl
from jax.experimental.pallas import tpu as pltpu
from jax.sharding import PartitionSpec as P

ITERS = 2
SEED_GAIN = 4.0
EPS = 1e-05
B = 128
NB = 64
KN = 8
KA = 4
NA = 128
H = 2
R = B // H
PIECES = 4
STEP = 16
FORWARD_VMEM, REST_VMEM = 56, 50
F32 = jnp.float32
BF16 = jnp.bfloat16
MESH = pl.DeviceIdType.MESH


def place(ids):
    z, y, core, slot = ids >> 5, (ids >> 3) & 3, (ids >> 2) & 1, ids & 3
    first = z + core * (y - z)
    second = y + core * (z - y)
    return (core << 6) + (first << 4) + (second << 2) + slot


def forward_kernel(
    lists, seeds, scores_in, tiles_in, held, seeded_out,
    total, narrow, tiles, scores, seeded, out_sems, tile_sems, score_sems, seeded_sems,
):
    start_row = lax.axis_index("node") * (NB * B)
    rows_of = lambda g: pl.ds(pl.multiple_of(g * (STEP * B), STEP * B), STEP * B)
    blocks_of = lambda g: pl.ds(g * STEP, STEP)
    score_copy = lambda g: pltpu.make_async_copy(scores_in.at[rows_of(g)], scores.at[rows_of(g)], score_sems.at[g])
    tile_copy = lambda g: pltpu.make_async_copy(tiles_in.at[blocks_of(g)], tiles.at[blocks_of(g)], tile_sems.at[g])
    seeded_copy = lambda g: pltpu.make_async_copy(seeded.at[blocks_of(g)], seeded_out.at[blocks_of(g)], seeded_sems.at[g])
    for g in range(NB // STEP):
        score_copy(g).start()
        tile_copy(g).start()

    def clear(i, carry):
        for u in range(4):
            total[i * 4 + u] = jnp.zeros((B, B), F32)
        return carry

    lax.fori_loop(0, NA // 4, clear, 0)
    wanted = seeds[...]

    def group(g, carry):
        score_copy(g).wait()
        tile_copy(g).wait()
        for u in range(STEP):
            b = g * STEP + u
            at_rows = pl.ds(pl.multiple_of(b * B, B), B)
            rows = lax.broadcasted_iota(jnp.int32, (B, B), 0) + (start_row + b * B)
            hit = (rows == wanted).astype(F32)
            block = scores[at_rows, :].astype(F32) + SEED_GAIN * hit
            flipped = block.astype(BF16).T
            seeded[b] = flipped
            for k in range(KN):
                term = jnp.dot(flipped, tiles[b, k], preferred_element_type=F32)
                total[place(lists[k, b])] += term
        seeded_copy(g).start()
        return carry

    lax.fori_loop(0, NB // STEP, group, 0)
    copies = []
    for c in range(PIECES):

        def body(i, carry):
            for u in range(4):
                a = c * (NA // PIECES) + i * 4 + u
                whole = total[a].astype(BF16)
                for h in range(H):
                    narrow[h, a] = whole[h * R : (h + 1) * R]
            return carry

        lax.fori_loop(0, NA // PIECES // 4, body, 0)
        at = pl.ds(c * (NA // PIECES), NA // PIECES)
        for h in range(H):
            copy = pltpu.make_async_copy(narrow.at[h, at], held.at[h, at], out_sems.at[c * H + h])
            copy.start()
            copies.append(copy)
    for copy in copies:
        copy.wait()
    for g in range(NB // STEP):
        seeded_copy(g).wait()


def forward(lists, seeds, scores, tiles):
    hbm = pl.BlockSpec(memory_space=pl.ANY)
    sems = pltpu.SemaphoreType.DMA
    return pl.pallas_call(
        forward_kernel,
        in_specs=[pl.BlockSpec(memory_space=pltpu.SMEM), pl.BlockSpec(memory_space=pltpu.VMEM), hbm, hbm],
        out_specs=[hbm, hbm],
        out_shape=[
            jax.ShapeDtypeStruct((H, NA, R, B), BF16),
            jax.ShapeDtypeStruct((NB, B, B), BF16),
        ],
        scratch_shapes=[
            pltpu.VMEM((NA, B, B), F32),
            pltpu.VMEM((H, NA, R, B), BF16),
            pltpu.VMEM((NB, KN, B, B), BF16),
            pltpu.VMEM((NB * B, B), BF16),
            pltpu.VMEM((NB, B, B), BF16),
            sems((PIECES * H,)),
            sems((NB // STEP,)),
            sems((NB // STEP,)),
            sems((NB // STEP,)),
        ],
        compiler_params=pltpu.CompilerParams(vmem_limit_bytes=FORWARD_VMEM << 20),
        cost_estimate=pl.CostEstimate(flops=2 * NB * KN * B**3, bytes_accessed=24 << 20, transcendentals=0),
        name="forward",
    )(lists, seeds, scores, tiles)


CHUNKS = 4
PER = NB // CHUNKS
UNROLL = 16
RS_SEMS = 4 + 6 + 3
AG_SEMS = 3 + 6 + 4
HALF_SEMS = RS_SEMS + (ITERS + 1) * AG_SEMS
TILE_SEMS = 3 * 4


def rest_kernel(lists, near, held, seeded_in, atiles, tiles_in, rank_out, score_out, *scratch):
    scratch = list(scratch)
    take = lambda n: [scratch.pop(0) for _ in range(n)]
    tiles, seeded, resid, energy, others = take(5)
    own, mate = take(H), take(H)
    far, up, down, ra, rb, gm, gp = (take(H) for _ in range(7))
    out2, in2 = take(H), take(H)
    sums, values = take(H), take(H)
    (row_tiles,) = take(1)
    shared = [take(H) for _ in range(ITERS + 1)]
    send_sems, recv_sems, local_sems, esend, erecv = take(5)

    node, pb = lax.axis_index("node"), lax.axis_index("pb")
    core = node % 2
    sf, ss = 8 - 6 * core, 2 + 6 * core
    pf, ps = (node // sf) % 4, (node // ss) % 4
    turn = lambda at, by: (at + by + 4) % 4
    f_up = node + (turn(pf, 1) - pf) * sf
    f_dn = node + (turn(pf, -1) - pf) * sf
    s_up = node + (turn(ps, 1) - ps) * ss
    s_dn = node + (turn(ps, -1) - ps) * ss
    s_far = node + (turn(ps, 2) - ps) * ss
    ring = ((2, s_far), (1, s_up), (-1, s_dn))
    sib = node + 1 - 2 * core

    locals_ = []

    def local(src, dst):
        copy = pltpu.make_async_copy(src, dst, local_sems.at[len(locals_)])
        copy.start()
        locals_.append(copy)
        return copy

    own_copies = [local(held.at[h, pl.ds(core * 64, 64)], own[h]) for h in range(H)]
    own_tiles_copy = local(atiles, row_tiles.at[ps])
    seeded_copy = local(seeded_in, seeded)
    load_tiles = lambda: [
        local(tiles_in.at[pl.ds(i * PER, PER)], tiles.at[pl.ds(i * PER, PER)]) for i in range(CHUNKS)
    ]

    barrier = pltpu.get_barrier_semaphore()
    for peer in (sib, f_up, f_dn, s_up, s_dn, s_far):
        pl.semaphore_signal(barrier, inc=1, device_id={"node": peer}, device_id_type=MESH)
    for by in (1, 2, 3):
        pl.semaphore_signal(barrier, inc=1, device_id={"pb": turn(pb, by)}, device_id_type=MESH)
    pl.semaphore_wait(barrier, 9)

    started = []
    count = [0] * (H + 1)

    def send(h, src, dst, peer):
        i = h * HALF_SEMS + count[h]
        count[h] += 1
        copy = pltpu.make_async_remote_copy(
            src_ref=src, dst_ref=dst, send_sem=send_sems.at[i], recv_sem=recv_sems.at[i],
            device_id=peer if isinstance(peer, dict) else {"node": peer}, device_id_type=MESH,
        )
        copy.start()
        started.append(copy)
        return copy

    def pass_tiles_on():
        for copy in tile_hops:
            copy.wait_recv()
        return [
            send(H, row_tiles.at[turn(ps, by), pb], row_tiles.at[turn(ps, by), pb], {"pb": turn(pb, d)})
            for by, _ in ring for d in (1, 2, 3)
        ]

    def add_blocks(n, dst, dst_at, *terms):
        def body(i, carry):
            for u in range(4):
                j = i * 4 + u
                acc = terms[0][0][terms[0][1] + j].astype(F32)
                for ref, at in terms[1:]:
                    acc = acc + ref[at + j].astype(F32)
                dst[dst_at + j] = acc.astype(dst.dtype)
            return carry

        lax.fori_loop(0, n // 4, body, 0)

    def reduce_scatter(h):
        o, m = own[h], mate[h]
        other = (1 - core) * 64
        got = {}
        for by in (2, 1, 3, 0):
            f = turn(ps, by)
            got[by] = send(h, held.at[h, pl.ds(other + f * 16, 16)], m.at[pl.ds(f * 16, 16)], sib)
        yield
        own_copies[h].wait()
        got[2].wait_recv()
        at = turn(pf, 2) * 16
        add_blocks(16, far[h], 0, (o, at), (m, at))
        a1 = send(h, far[h].at[pl.ds(0, 8)], ra[h], f_up)
        b1 = send(h, far[h].at[pl.ds(8, 8)], rb[h], f_dn)
        at_up, at_dn = turn(pf, 1) * 16, turn(pf, -1) * 16
        got[1].wait_recv()
        add_blocks(8, up[h], 8, (o, at_up + 8), (m, at_up + 8))
        mb = send(h, up[h].at[pl.ds(8, 8)], gm[h].at[pl.ds(8, 8)], f_up)
        got[3].wait_recv()
        add_blocks(8, down[h], 0, (o, at_dn), (m, at_dn))
        pa = send(h, down[h].at[pl.ds(0, 8)], gp[h].at[pl.ds(0, 8)], f_dn)
        yield
        a1.wait_recv()
        add_blocks(8, up[h], 0, (o, at_up), (m, at_up), (ra[h], 0))
        ma = send(h, up[h].at[pl.ds(0, 8)], gm[h].at[pl.ds(0, 8)], f_up)
        b1.wait_recv()
        add_blocks(8, down[h], 8, (o, at_dn + 8), (m, at_dn + 8), (rb[h], 0))
        pb_ = send(h, down[h].at[pl.ds(8, 8)], gp[h].at[pl.ds(8, 8)], f_dn)
        yield
        got[0].wait_recv()
        for copy in (mb, pa, ma, pb_):
            copy.wait_recv()
        mine = pf * 16

        def part(s, skip):
            at = s * 4 + skip
            return (o, mine + at), (m, mine + at), (gm[h], at), (gp[h], at)

        hops = []
        for by, peer in ring:
            to = turn(ps, by) * 4
            add_blocks(4, out2[h], to, *part(turn(ps, by), 0))
            hops.append(send(h, out2[h].at[pl.ds(to, 4)], in2[h].at[ps], peer))
        yield
        add_blocks(4, sums[h], ps * 4, *part(ps, 0))
        for copy in hops:
            copy.wait_recv()
        for by in (2, 1, 3):
            add_blocks(4, sums[h], ps * 4, (sums[h], ps * 4), (in2[h].at[turn(ps, by)], 0))

    def all_gather(h, buf, whole):
        base = core * 64
        row = base + pf * 16
        mine = row + ps * 4
        at = lambda start, n: buf.at[pl.ds(start, n)]
        go = lambda start, n, peer: send(h, at(start, n), at(start, n), peer)
        if not whole:
            hops = [go(mine, 4, peer) for _, peer in ring]
            yield
            for copy in hops:
                copy.wait_recv()
        ua = go(row, 8, f_up)
        db = go(row + 8, 8, f_dn)
        ub = go(row + 8, 8, f_up)
        da = go(row, 8, f_dn)
        across = [go(row, 16, sib)]
        yield
        low, high, far_ = base + turn(pf, -1) * 16, base + turn(pf, 1) * 16, base + turn(pf, 2) * 16
        ua.wait_recv()
        ua2 = go(low, 8, f_up)
        db.wait_recv()
        db2 = go(high + 8, 8, f_dn)
        ub.wait_recv()
        across.append(go(low, 16, sib))
        da.wait_recv()
        across.append(go(high, 16, sib))
        yield
        ua2.wait_recv()
        db2.wait_recv()
        across.append(go(far_, 16, sib))
        for copy in across:
            copy.wait_recv()

    def iterate(h, buf, out):
        row = core * 64 + pf * 16

        def body(s, carry):
            anchors = (node + (s - ps) * ss) * 4
            for r in range(4):
                acc = sums[h][s * 4 + r]
                for k in range(0, KA, 2):
                    left = jnp.concatenate([buf[place(near[k + i, anchors + r])] for i in range(2)], axis=1)
                    right = jnp.concatenate([row_tiles[s, r, k + i] for i in range(2)], axis=1)
                    acc = acc + lax.dot_general(left, right, (((1,), (1,)), ((), ())), preferred_element_type=F32)
                values[h][s * 4 + r] = acc
                out[row + s * 4 + r] = acc.astype(BF16)
            return carry

        lax.fori_loop(0, 4, body, 0)

    def pipeline(h):
        yield from reduce_scatter(h)
        row = core * 64 + pf * 16
        add_blocks(4, shared[0][h], row + ps * 4, (sums[h], ps * 4))
        yield from all_gather(h, shared[0][h], False)
        for by, _ in ring:
            at = turn(ps, by) * 4
            add_blocks(4, sums[h], at, (shared[0][h], row + at))
        if h == 0:
            for copy in tile_passes:
                copy.wait_recv()
            own_tiles_copy.wait()
        for t in range(ITERS):
            iterate(h, shared[t][h], shared[t + 1][h])
            yield from all_gather(h, shared[t + 1][h], True)

    lines = [pipeline(h) for h in range(H)]
    live = list(range(H))
    for line in lines:
        next(line)
    tile_hops = [send(H, atiles.at[pb], row_tiles.at[ps, pb], peer) for _, peer in ring]
    for line in lines:
        next(line)
    tile_passes = pass_tiles_on()
    tile_copies = load_tiles()
    while live:
        for h in list(live):
            try:
                next(lines[h])
            except StopIteration:
                live.remove(h)

    for r in range(4):
        whole = jnp.concatenate([values[h][ps * 4 + r] for h in range(H)], axis=0)
        score_out[r * B : (r + 1) * B, :] = whole.T

    seeded_copy.wait()
    final = shared[ITERS]
    esends = []

    def finish(c):
        for copy in esends[c]:
            copy.wait_recv()

        def body(i, carry):
            for u in range(UNROLL):
                b = c * PER + i * UNROLL + u
                tot = energy[pl.ds(b, 1), :]
                for d in range(3):
                    tot = tot + others[d, pl.ds(b, 1), :]
                scale = lax.rsqrt(tot / 512.0 + EPS)
                block = (resid[b] * scale).astype(BF16)
                rank_out[pl.ds(pl.multiple_of(b * B, B), B), :] = block.T
            return carry

        lax.fori_loop(0, PER // UNROLL, body, 0)

    for c in range(CHUNKS):
        tile_copies[c].wait()

        def body(i, carry):
            for u in range(UNROLL):
                b = c * PER + i * UNROLL + u
                acc = None
                for k in range(0, KN, 2):
                    pieces = []
                    for j in range(2):
                        at = place(lists[k + j, b])
                        pieces.append(jnp.concatenate([final[h][at] for h in range(H)], axis=0))
                    left = jnp.concatenate(pieces, axis=1)
                    right = jnp.concatenate([tiles[b, k + j] for j in range(2)], axis=1)
                    part = lax.dot_general(left, right, (((1,), (1,)), ((), ())), preferred_element_type=F32)
                    acc = part if acc is None else acc + part
                res = seeded[b].astype(F32) - acc
                resid[b] = res
                energy[pl.ds(b, 1), :] = jnp.sum(res * res, axis=0, keepdims=True)
            return carry

        lax.fori_loop(0, PER // UNROLL, body, 0)
        group = []
        for d in (1, 2, 3):
            i = c * 3 + d - 1
            copy = pltpu.make_async_remote_copy(
                src_ref=energy.at[pl.ds(c * PER, PER)], dst_ref=others.at[d - 1, pl.ds(c * PER, PER)],
                send_sem=esend.at[i], recv_sem=erecv.at[i],
                device_id={"pb": turn(pb, d)}, device_id_type=MESH,
            )
            copy.start()
            group.append(copy)
        esends.append(group)
    for c in range(CHUNKS):
        finish(c)

    for copy in started:
        copy.wait_send()
    for group in esends:
        for copy in group:
            copy.wait_send()


def rest(lists, near, held, seeded, atiles, tiles):
    vm = lambda *shape, dtype=BF16: pltpu.VMEM(shape, dtype)
    per_half = lambda n, dtype=BF16: [pltpu.VMEM((n, R, B), dtype) for _ in range(H)]
    scratch = [
        vm(NB, KN, B, B),
        vm(NB, B, B),
        vm(NB, B, B, dtype=F32),
        vm(NB, B, dtype=F32),
        vm(3, NB, B, dtype=F32),
    ]
    for n in (64, 64, 16, 16, 16, 8, 8, 16, 16, 16):
        scratch += per_half(n)
    scratch += [vm(4, 4, R, B) for _ in range(H)]
    scratch += per_half(16, F32) + per_half(16, F32)
    scratch += [vm(4, 4, KA, B, B)]
    for _ in range(ITERS + 1):
        scratch += per_half(NA)
    sems = pltpu.SemaphoreType.DMA
    scratch += [
        sems((H * HALF_SEMS + TILE_SEMS,)), sems((H * HALF_SEMS + TILE_SEMS,)), sems((H + 2 + CHUNKS,)),
        sems((3 * CHUNKS,)), sems((3 * CHUNKS,)),
    ]
    smem = pl.BlockSpec(memory_space=pltpu.SMEM)
    vmem = pl.BlockSpec(memory_space=pltpu.VMEM)
    hbm = pl.BlockSpec(memory_space=pl.ANY)
    return pl.pallas_call(
        rest_kernel,
        in_specs=[smem, smem, hbm, hbm, hbm, hbm],
        out_specs=[vmem, vmem],
        out_shape=[jax.ShapeDtypeStruct((NB * B, B), BF16), jax.ShapeDtypeStruct((4 * B, B), F32)],
        scratch_shapes=scratch,
        compiler_params=pltpu.CompilerParams(
            collective_id=0, has_side_effects=True, vmem_limit_bytes=REST_VMEM << 20
        ),
        cost_estimate=pl.CostEstimate(flops=2 * NB * KN * B**3, bytes_accessed=28 << 20, transcendentals=0),
        name="rest",
    )(lists, near, held, seeded, atiles, tiles)


def shards(node_scores, seeds, node_lists, node_tiles, anchor_lists, anchor_tiles):
    lists = node_lists.T
    held, seeded = forward(lists, seeds.reshape(1, B), node_scores, node_tiles)
    ranking, anchor_scores = rest(lists, anchor_lists.T, held, seeded, anchor_tiles, node_tiles)
    return (ranking, anchor_scores)


def solution(mesh):
    in_specs = (
        P("node", "pb"),
        P("pb"),
        P("node", None),
        P("node", None, None, None),
        P(),
        P("node", None, None, None),
    )
    out_specs = (P("node", "pb"), P("node", "pb"))
    return jax.shard_map(shards, mesh=mesh, in_specs=in_specs, out_specs=out_specs, check_vma=False)
```

```python
import functools

import jax
import jax.numpy as jnp
from jax import lax
from jax.experimental import pallas as pl
from jax.experimental.pallas import tpu as pltpu
from jax.sharding import PartitionSpec as P

ITERS = 2
SEED_GAIN = 4.0
EPS = 1e-05
B = 128
NB = 64
KN = 8
KA = 4
NA = 128
H = 2
R = B // H
PIECES = 4
STEP = 16
FORWARD_VMEM, REST_VMEM = 56, 50
F32 = jnp.float32
BF16 = jnp.bfloat16
MESH = pl.DeviceIdType.MESH


def place(ids):
    z, y, core, slot = ids >> 5, (ids >> 3) & 3, (ids >> 2) & 1, ids & 3
    first = z + core * (y - z)
    second = y + core * (z - y)
    return (core << 6) + (first << 4) + (second << 2) + slot


def forward_kernel(
    lists, seeds, scores_in, tiles_in, held, seeded_out,
    total, narrow, tiles, scores, seeded, out_sems, tile_sems, score_sems, seeded_sems,
):
    start_row = lax.axis_index("node") * (NB * B)
    rows_of = lambda g: pl.ds(pl.multiple_of(g * (STEP * B), STEP * B), STEP * B)
    blocks_of = lambda g: pl.ds(g * STEP, STEP)
    score_copy = lambda g: pltpu.make_async_copy(scores_in.at[rows_of(g)], scores.at[rows_of(g)], score_sems.at[g])
    tile_copy = lambda g: pltpu.make_async_copy(tiles_in.at[blocks_of(g)], tiles.at[blocks_of(g)], tile_sems.at[g])
    seeded_copy = lambda g: pltpu.make_async_copy(seeded.at[blocks_of(g)], seeded_out.at[blocks_of(g)], seeded_sems.at[g])
    for g in range(NB // STEP):
        score_copy(g).start()
        tile_copy(g).start()

    def clear(i, carry):
        for u in range(4):
            total[i * 4 + u] = jnp.zeros((B, B), F32)
        return carry

    lax.fori_loop(0, NA // 4, clear, 0)
    wanted = seeds[...]

    def group(g, carry):
        score_copy(g).wait()
        tile_copy(g).wait()
        for u in range(STEP):
            b = g * STEP + u
            at_rows = pl.ds(pl.multiple_of(b * B, B), B)
            rows = lax.broadcasted_iota(jnp.int32, (B, B), 0) + (start_row + b * B)
            hit = (rows == wanted).astype(F32)
            block = scores[at_rows, :].astype(F32) + SEED_GAIN * hit
            flipped = block.astype(BF16).T
            seeded[b] = flipped
            for k in range(KN):
                term = jnp.dot(flipped, tiles[b, k], preferred_element_type=F32)
                total[place(lists[k, b])] += term
        seeded_copy(g).start()
        return carry

    lax.fori_loop(0, NB // STEP, group, 0)
    copies = []
    for c in range(PIECES):

        def body(i, carry):
            for u in range(4):
                a = c * (NA // PIECES) + i * 4 + u
                whole = total[a].astype(BF16)
                for h in range(H):
                    narrow[h, a] = whole[h * R : (h + 1) * R]
            return carry

        lax.fori_loop(0, NA // PIECES // 4, body, 0)
        at = pl.ds(c * (NA // PIECES), NA // PIECES)
        for h in range(H):
            copy = pltpu.make_async_copy(narrow.at[h, at], held.at[h, at], out_sems.at[c * H + h])
            copy.start()
            copies.append(copy)
    for copy in copies:
        copy.wait()
    for g in range(NB // STEP):
        seeded_copy(g).wait()


def forward(lists, seeds, scores, tiles):
    hbm = pl.BlockSpec(memory_space=pl.ANY)
    sems = pltpu.SemaphoreType.DMA
    return pl.pallas_call(
        forward_kernel,
        in_specs=[pl.BlockSpec(memory_space=pltpu.SMEM), pl.BlockSpec(memory_space=pltpu.VMEM), hbm, hbm],
        out_specs=[hbm, hbm],
        out_shape=[
            jax.ShapeDtypeStruct((H, NA, R, B), BF16),
            jax.ShapeDtypeStruct((NB, B, B), BF16),
        ],
        scratch_shapes=[
            pltpu.VMEM((NA, B, B), F32),
            pltpu.VMEM((H, NA, R, B), BF16),
            pltpu.VMEM((NB, KN, B, B), BF16),
            pltpu.VMEM((NB * B, B), BF16),
            pltpu.VMEM((NB, B, B), BF16),
            sems((PIECES * H,)),
            sems((NB // STEP,)),
            sems((NB // STEP,)),
            sems((NB // STEP,)),
        ],
        compiler_params=pltpu.CompilerParams(vmem_limit_bytes=FORWARD_VMEM << 20),
        cost_estimate=pl.CostEstimate(flops=2 * NB * KN * B**3, bytes_accessed=24 << 20, transcendentals=0),
        name="forward",
    )(lists, seeds, scores, tiles)


CHUNKS = 4
PER = NB // CHUNKS
UNROLL = 16
RS_SEMS = 4 + 6 + 3
AG_SEMS = 3 + 6 + 4
HALF_SEMS = RS_SEMS + (ITERS + 1) * AG_SEMS
TILE_SEMS = 3 * 4


def rest_kernel(lists, near, held, seeded_in, atiles, tiles_in, rank_out, score_out, *scratch):
    scratch = list(scratch)
    take = lambda n: [scratch.pop(0) for _ in range(n)]
    tiles, seeded, resid, energy, others = take(5)
    own, mate = take(H), take(H)
    far, up, down, ra, rb, gm, gp = (take(H) for _ in range(7))
    out2, in2 = take(H), take(H)
    sums, values = take(H), take(H)
    (row_tiles,) = take(1)
    shared = [take(H) for _ in range(ITERS + 1)]
    send_sems, recv_sems, local_sems, esend, erecv = take(5)

    node, pb = lax.axis_index("node"), lax.axis_index("pb")
    core = node % 2
    sf, ss = 8 - 6 * core, 2 + 6 * core
    pf, ps = (node // sf) % 4, (node // ss) % 4
    turn = lambda at, by: (at + by + 4) % 4
    f_up = node + (turn(pf, 1) - pf) * sf
    f_dn = node + (turn(pf, -1) - pf) * sf
    s_up = node + (turn(ps, 1) - ps) * ss
    s_dn = node + (turn(ps, -1) - ps) * ss
    s_far = node + (turn(ps, 2) - ps) * ss
    ring = ((2, s_far), (1, s_up), (-1, s_dn))
    sib = node + 1 - 2 * core

    locals_ = []

    def local(src, dst):
        copy = pltpu.make_async_copy(src, dst, local_sems.at[len(locals_)])
        copy.start()
        locals_.append(copy)
        return copy

    own_copies = [local(held.at[h, pl.ds(core * 64, 64)], own[h]) for h in range(H)]
    own_tiles_copy = local(atiles, row_tiles.at[ps])
    seeded_copy = local(seeded_in, seeded)
    load_tiles = lambda: [
        local(tiles_in.at[pl.ds(i * PER, PER)], tiles.at[pl.ds(i * PER, PER)]) for i in range(CHUNKS)
    ]

    barrier = pltpu.get_barrier_semaphore()
    for peer in (sib, f_up, f_dn, s_up, s_dn, s_far):
        pl.semaphore_signal(barrier, inc=1, device_id={"node": peer}, device_id_type=MESH)
    for by in (1, 2, 3):
        pl.semaphore_signal(barrier, inc=1, device_id={"pb": turn(pb, by)}, device_id_type=MESH)
    pl.semaphore_wait(barrier, 9)

    started = []
    count = [0] * (H + 1)

    def send(h, src, dst, peer):
        i = h * HALF_SEMS + count[h]
        count[h] += 1
        copy = pltpu.make_async_remote_copy(
            src_ref=src, dst_ref=dst, send_sem=send_sems.at[i], recv_sem=recv_sems.at[i],
            device_id=peer if isinstance(peer, dict) else {"node": peer}, device_id_type=MESH,
        )
        copy.start()
        started.append(copy)
        return copy

    def pass_tiles_on():
        for copy in tile_hops:
            copy.wait_recv()
        return [
            send(H, row_tiles.at[turn(ps, by), pb], row_tiles.at[turn(ps, by), pb], {"pb": turn(pb, d)})
            for by, _ in ring for d in (1, 2, 3)
        ]

    def add_blocks(n, dst, dst_at, *terms):
        def body(i, carry):
            for u in range(4):
                j = i * 4 + u
                acc = terms[0][0][terms[0][1] + j].astype(F32)
                for ref, at in terms[1:]:
                    acc = acc + ref[at + j].astype(F32)
                dst[dst_at + j] = acc.astype(dst.dtype)
            return carry

        lax.fori_loop(0, n // 4, body, 0)

    def reduce_scatter(h):
        o, m = own[h], mate[h]
        other = (1 - core) * 64
        got = {}
        for by in (2, 1, 3, 0):
            f = turn(ps, by)
            got[by] = send(h, held.at[h, pl.ds(other + f * 16, 16)], m.at[pl.ds(f * 16, 16)], sib)
        yield
        own_copies[h].wait()
        got[2].wait_recv()
        at = turn(pf, 2) * 16
        add_blocks(16, far[h], 0, (o, at), (m, at))
        a1 = send(h, far[h].at[pl.ds(0, 8)], ra[h], f_up)
        b1 = send(h, far[h].at[pl.ds(8, 8)], rb[h], f_dn)
        yield
        at_up, at_dn = turn(pf, 1) * 16, turn(pf, -1) * 16
        got[1].wait_recv()
        add_blocks(8, up[h], 8, (o, at_up + 8), (m, at_up + 8))
        mb = send(h, up[h].at[pl.ds(8, 8)], gm[h].at[pl.ds(8, 8)], f_up)
        got[3].wait_recv()
        add_blocks(8, down[h], 0, (o, at_dn), (m, at_dn))
        pa = send(h, down[h].at[pl.ds(0, 8)], gp[h].at[pl.ds(0, 8)], f_dn)
        yield
        a1.wait_recv()
        add_blocks(8, up[h], 0, (o, at_up), (m, at_up), (ra[h], 0))
        ma = send(h, up[h].at[pl.ds(0, 8)], gm[h].at[pl.ds(0, 8)], f_up)
        b1.wait_recv()
        add_blocks(8, down[h], 8, (o, at_dn + 8), (m, at_dn + 8), (rb[h], 0))
        pb_ = send(h, down[h].at[pl.ds(8, 8)], gp[h].at[pl.ds(8, 8)], f_dn)
        yield
        got[0].wait_recv()
        for copy in (mb, pa, ma, pb_):
            copy.wait_recv()
        mine = pf * 16

        def part(s, skip):
            at = s * 4 + skip
            return (o, mine + at), (m, mine + at), (gm[h], at), (gp[h], at)

        hops = []
        for by, peer in ring:
            to = turn(ps, by) * 4
            add_blocks(4, out2[h], to, *part(turn(ps, by), 0))
            hops.append(send(h, out2[h].at[pl.ds(to, 4)], in2[h].at[ps], peer))
        yield
        add_blocks(4, sums[h], ps * 4, *part(ps, 0))
        for copy in hops:
            copy.wait_recv()
        for by in (2, 1, 3):
            add_blocks(4, sums[h], ps * 4, (sums[h], ps * 4), (in2[h].at[turn(ps, by)], 0))

    def all_gather(h, buf, whole):
        base = core * 64
        row = base + pf * 16
        mine = row + ps * 4
        at = lambda start, n: buf.at[pl.ds(start, n)]
        go = lambda start, n, peer: send(h, at(start, n), at(start, n), peer)
        if not whole:
            hops = [go(mine, 4, peer) for _, peer in ring]
            yield
            for copy in hops:
                copy.wait_recv()
        ua = go(row, 8, f_up)
        db = go(row + 8, 8, f_dn)
        ub = go(row + 8, 8, f_up)
        da = go(row, 8, f_dn)
        across = [go(row, 16, sib)]
        yield
        low, high, far_ = base + turn(pf, -1) * 16, base + turn(pf, 1) * 16, base + turn(pf, 2) * 16
        ua.wait_recv()
        ua2 = go(low, 8, f_up)
        db.wait_recv()
        db2 = go(high + 8, 8, f_dn)
        ub.wait_recv()
        across.append(go(low, 16, sib))
        da.wait_recv()
        across.append(go(high, 16, sib))
        yield
        ua2.wait_recv()
        db2.wait_recv()
        across.append(go(far_, 16, sib))
        for copy in across:
            copy.wait_recv()

    def iterate(h, buf, out):
        row = core * 64 + pf * 16

        def body(s, carry):
            anchors = (node + (s - ps) * ss) * 4
            for r in range(4):
                acc = sums[h][s * 4 + r]
                for k in range(0, KA, 2):
                    left = jnp.concatenate([buf[place(near[k + i, anchors + r])] for i in range(2)], axis=1)
                    right = jnp.concatenate([row_tiles[s, r, k + i] for i in range(2)], axis=1)
                    acc = acc + lax.dot_general(left, right, (((1,), (1,)), ((), ())), preferred_element_type=F32)
                values[h][s * 4 + r] = acc
                out[row + s * 4 + r] = acc.astype(BF16)
            return carry

        lax.fori_loop(0, 4, body, 0)

    def pipeline(h):
        yield from reduce_scatter(h)
        row = core * 64 + pf * 16
        add_blocks(4, shared[0][h], row + ps * 4, (sums[h], ps * 4))
        yield from all_gather(h, shared[0][h], False)
        for by, _ in ring:
            at = turn(ps, by) * 4
            add_blocks(4, sums[h], at, (shared[0][h], row + at))
        if h == 0:
            for copy in tile_passes:
                copy.wait_recv()
            own_tiles_copy.wait()
        for t in range(ITERS):
            iterate(h, shared[t][h], shared[t + 1][h])
            yield from all_gather(h, shared[t + 1][h], True)

    lines = [pipeline(h) for h in range(H)]
    live = list(range(H))
    for turn_no in range(1):
        for line in lines:
            next(line)
    tile_hops = [send(H, atiles.at[pb], row_tiles.at[ps, pb], peer) for _, peer in ring]
    for turn_no in range(3):
        for line in lines:
            next(line)
    tile_passes = pass_tiles_on()
    tile_copies = load_tiles()
    while live:
        for h in list(live):
            try:
                next(lines[h])
            except StopIteration:
                live.remove(h)

    for r in range(4):
        whole = jnp.concatenate([values[h][ps * 4 + r] for h in range(H)], axis=0)
        score_out[r * B : (r + 1) * B, :] = whole.T

    seeded_copy.wait()
    final = shared[ITERS]
    esends = []

    def finish(c):
        for copy in esends[c]:
            copy.wait_recv()

        def body(i, carry):
            for u in range(UNROLL):
                b = c * PER + i * UNROLL + u
                tot = energy[pl.ds(b, 1), :]
                for d in range(3):
                    tot = tot + others[d, pl.ds(b, 1), :]
                scale = lax.rsqrt(tot / 512.0 + EPS)
                block = (resid[b] * scale).astype(BF16)
                rank_out[pl.ds(pl.multiple_of(b * B, B), B), :] = block.T
            return carry

        lax.fori_loop(0, PER // UNROLL, body, 0)

    for c in range(CHUNKS):
        tile_copies[c].wait()

        def body(i, carry):
            for u in range(UNROLL):
                b = c * PER + i * UNROLL + u
                acc = None
                for k in range(0, KN, 2):
                    pieces = []
                    for j in range(2):
                        at = place(lists[k + j, b])
                        pieces.append(jnp.concatenate([final[h][at] for h in range(H)], axis=0))
                    left = jnp.concatenate(pieces, axis=1)
                    right = jnp.concatenate([tiles[b, k + j] for j in range(2)], axis=1)
                    part = lax.dot_general(left, right, (((1,), (1,)), ((), ())), preferred_element_type=F32)
                    acc = part if acc is None else acc + part
                res = seeded[b].astype(F32) - acc
                resid[b] = res
                energy[pl.ds(b, 1), :] = jnp.sum(res * res, axis=0, keepdims=True)
            return carry

        lax.fori_loop(0, PER // UNROLL, body, 0)
        group = []
        for d in (1, 2, 3):
            i = c * 3 + d - 1
            copy = pltpu.make_async_remote_copy(
                src_ref=energy.at[pl.ds(c * PER, PER)], dst_ref=others.at[d - 1, pl.ds(c * PER, PER)],
                send_sem=esend.at[i], recv_sem=erecv.at[i],
                device_id={"pb": turn(pb, d)}, device_id_type=MESH,
            )
            copy.start()
            group.append(copy)
        esends.append(group)
    for c in range(CHUNKS):
        finish(c)

    for copy in started:
        copy.wait_send()
    for group in esends:
        for copy in group:
            copy.wait_send()


def rest(lists, near, held, seeded, atiles, tiles):
    vm = lambda *shape, dtype=BF16: pltpu.VMEM(shape, dtype)
    per_half = lambda n, dtype=BF16: [pltpu.VMEM((n, R, B), dtype) for _ in range(H)]
    scratch = [
        vm(NB, KN, B, B),
        vm(NB, B, B),
        vm(NB, B, B, dtype=F32),
        vm(NB, B, dtype=F32),
        vm(3, NB, B, dtype=F32),
    ]
    for n in (64, 64, 16, 16, 16, 8, 8, 16, 16, 16):
        scratch += per_half(n)
    scratch += [vm(4, 4, R, B) for _ in range(H)]
    scratch += per_half(16, F32) + per_half(16, F32)
    scratch += [vm(4, 4, KA, B, B)]
    for _ in range(ITERS + 1):
        scratch += per_half(NA)
    sems = pltpu.SemaphoreType.DMA
    scratch += [
        sems((H * HALF_SEMS + TILE_SEMS,)), sems((H * HALF_SEMS + TILE_SEMS,)), sems((H + 2 + CHUNKS,)),
        sems((3 * CHUNKS,)), sems((3 * CHUNKS,)),
    ]
    smem = pl.BlockSpec(memory_space=pltpu.SMEM)
    vmem = pl.BlockSpec(memory_space=pltpu.VMEM)
    hbm = pl.BlockSpec(memory_space=pl.ANY)
    return pl.pallas_call(
        rest_kernel,
        in_specs=[smem, smem, hbm, hbm, hbm, hbm],
        out_specs=[vmem, vmem],
        out_shape=[jax.ShapeDtypeStruct((NB * B, B), BF16), jax.ShapeDtypeStruct((4 * B, B), F32)],
        scratch_shapes=scratch,
        compiler_params=pltpu.CompilerParams(
            collective_id=0, has_side_effects=True, vmem_limit_bytes=REST_VMEM << 20
        ),
        cost_estimate=pl.CostEstimate(flops=2 * NB * KN * B**3, bytes_accessed=28 << 20, transcendentals=0),
        name="rest",
    )(lists, near, held, seeded, atiles, tiles)


def shards(node_scores, seeds, node_lists, node_tiles, anchor_lists, anchor_tiles):
    lists = node_lists.T
    held, seeded = forward(lists, seeds.reshape(1, B), node_scores, node_tiles)
    ranking, anchor_scores = rest(lists, anchor_lists.T, held, seeded, anchor_tiles, node_tiles)
    return (ranking, anchor_scores)


def solution(mesh):
    in_specs = (
        P("node", "pb"),
        P("pb"),
        P("node", None),
        P("node", None, None, None),
        P(),
        P("node", None, None, None),
    )
    out_specs = (P("node", "pb"), P("node", "pb"))
    return jax.shard_map(shards, mesh=mesh, in_specs=in_specs, out_specs=out_specs, check_vma=False)
```
